32 devices in a mesh: seq: 16 (over z, y, x), tp: 2 (over core).
Axes of the slice: x: 2, y: 2, z: 4, core: 2. Of those that a mesh axis runs over, the one named last changes fastest.
Arguments:
- tokens: bfloat16 [1088, 2048], P('seq'), may hold values from -6 to 6
- norm_gain: bfloat16 [2048], replicated, may hold values from 0.099609375 to 1.8984375
- w_query: bfloat16 [2048, 2048], P(None, 'tp'), may hold values from -0.125 to 0.125
- w_key: bfloat16 [2048, 1024], P(None, 'tp'), may hold values from -0.125 to 0.125
- w_value: bfloat16 [2048, 1024], P(None, 'tp'), may hold values from -0.125 to 0.125
- w_out: bfloat16 [2048, 2048], P('tp'), may hold values from -0.125 to 0.125
- cache_keys: bfloat16 [32768, 1024], P('seq', 'tp'), may hold values from -400 to 400
- cache_values: bfloat16 [32768, 1024], P('seq', 'tp'), may hold values from -6 to 6
- cached_len: int32 [66], replicated, may hold values from 1 to 4096, 32768 in all
- block_of_shard: int32 [16], P('seq'), may hold values from 0 to 15, each once
Outputs:
- mixed: bfloat16 [1088, 2048], P('seq', 'tp')
The draws below stay inside these ranges and needn't reach their ends.
Inputs may be any that keep to these rules, and one draw needn't show every extreme that they name: `cached_len`: they sum to exactly 32768, so every cache slot belongs to a request; the largest is 4096. `block_of_shard`: each index of seq stores a different block.
All inputs are finite; a program needn't handle non-finite values.
Results may differ from the reference program's by a relative error of at most 0.02.
Values may be sent and summed in bfloat16 or wider, within the bound.
A program may use at most 192 MiB of HBM per device.

```python
import math
import jax
import jax.numpy as jnp
import numpy as np
from jax import lax

D = 2048
HQ = 16
KVH = 8
HD = 128
SPAN = 512
PREFILLS = 2
DECODES = 64
CACHE_DEV = 2048
NEW = 1088
REQS = 66
CACHE_ROWS = 32768
MAXLEN = 4096
N_SEQ = 16


def draw_cache_keys(key, part):
    first_key = jax.random.fold_in(key, 0)
    width_all = KVH * HD
    result = 1.5 * jax.random.normal(first_key, (CACHE_ROWS, width_all), jnp.float32)
    return result.astype(jnp.bfloat16)


def levels(own_key, extent, cuts, least, largest):
    loudness = 1.0
    for dim, parts in cuts:
        steps = jax.random.uniform(jax.random.fold_in(jax.random.fold_in(own_key, 6), dim), (parts,), jnp.float32, least / len(cuts), largest / len(cuts))
        loudness = loudness * jnp.repeat(jnp.exp(steps), extent[dim] // parts).reshape((-1,) + (1,) * (len(extent) - 1 - dim))
    return loudness


def length_profile(number_of, total, bound, slope):
    portions = [(1 << 20) // math.isqrt(rank ** slope) + 1 for rank in range(2, number_of + 1)]
    spare, counts = total - bound - (number_of - 1), [1] * (number_of - 1)
    while spare > 0:
        movable = [i for i in range(number_of - 1) if counts[i] < bound]
        whole, remaining = sum([portions[i] for i in movable]), spare
        for i in movable:
            more = min(bound - counts[i], max(1, remaining * portions[i] // whole), spare)
            counts[i] = counts[i] + more
            spare = spare - more
    return np.array([bound] + counts)


def ragged(own_key, number_of, total, bound, slope):
    if number_of == 2:
        one = jax.random.randint(own_key, (), max(1, total - bound), min(bound, total - 1) + 1)
        return jnp.stack([one, total - one])
    tallies = jnp.asarray(length_profile(number_of, total, bound, slope), jnp.int32)
    pairs = (number_of - 1) // 2
    giver, receiver = tallies[1:1 + 2 * pairs:2], tallies[2:2 + 2 * pairs:2]
    slack = jnp.minimum(giver - 1, bound - receiver)
    passed = jax.random.randint(jax.random.fold_in(own_key, 1), (pairs,), 0, 1 << 20) % (slack + 1)
    tallies = tallies.at[1:1 + 2 * pairs:2].set(giver - passed).at[2:2 + 2 * pairs:2].set(receiver + passed)
    return tallies[jax.random.permutation(jax.random.fold_in(own_key, 2), number_of)]


def bell_draw(own_key, dims, spread, bound, cuts=(), kind=jnp.bfloat16):
    drawn = spread * jax.random.normal(own_key, dims, jnp.float32)
    if cuts:
        drawn = drawn * levels(own_key, dims, cuts, -0.22, 0.18)
    return jnp.clip(drawn, -bound, bound).astype(kind)


def setup_inputs(seed: int = 0) -> dict:
    keys = jax.random.split(jax.random.key(seed), 11)
    return {
        "tokens": bell_draw(keys[0], (NEW, D), 1.0, 6.0, ((0, 16),)),
        "norm_gain": jnp.clip(1.0 + 0.18 * jax.random.normal(keys[1], (D,), jnp.float32), 0.099609375, 1.8984375).astype(jnp.bfloat16),
        "w_query": bell_draw(keys[2], (D, HQ * HD), D ** -0.5, 0.125, ((1, 2),)),
        "w_key": bell_draw(keys[3], (D, KVH * HD), D ** -0.5, 0.125, ((1, 2),)),
        "w_value": bell_draw(keys[4], (D, KVH * HD), D ** -0.5, 0.125, ((1, 2),)),
        "w_out": bell_draw(keys[5], (HQ * HD, D), (HQ * HD) ** -0.5, 0.125, ((0, 2),)),
        "cache_keys": draw_cache_keys(jax.random.fold_in(keys[10], 71), 0),
        "cache_values": bell_draw(keys[7], (CACHE_ROWS, KVH * HD), 1.0, 6.0, ((0, 16), (1, 2))),
        "cached_len": ragged(keys[8], REQS, CACHE_ROWS, MAXLEN, 2).astype(jnp.int32),
        "block_of_shard": jax.random.permutation(keys[9], N_SEQ).astype(jnp.int32),
    }


NEGATIVE = -1e+30
THETA = 1000000.0
EPSILON = 1e-06

def rotate(values, places):
    half_dim = values.shape[-1] // 2
    frequency = THETA ** (-jnp.arange(half_dim, dtype=jnp.float32) / half_dim)
    angles = places.astype(jnp.float32)[:, None] * frequency[None, :]
    cosine = jnp.cos(angles)[:, None, :]
    sine_part = jnp.sin(angles)[:, None, :]
    front_half = values[..., :half_dim]
    second = values[..., half_dim:]
    return jnp.concatenate([front_half * cosine - second * sine_part, second * cosine + front_half * sine_part], axis=-1)

def row_layout(row_count, cached_len):
    position_index = jnp.arange(row_count, dtype=jnp.int32)
    boundary = PREFILLS * SPAN
    request = jnp.where(position_index < boundary, position_index // SPAN, PREFILLS + position_index - boundary)
    offset = jnp.where(position_index < boundary, position_index % SPAN, 0)
    request = request.astype(jnp.int32)
    return (request, (jnp.take(cached_len, request) + offset).astype(jnp.int32))

def reference(tokens, norm_gain, w_query, w_key, w_value, w_out, cache_keys, cache_values, cached_len, block_of_shard):
    request, places = row_layout(NEW, cached_len)
    hidden = tokens.astype(jnp.float32)
    scale_row = lax.rsqrt(lax.optimization_barrier(jnp.mean(hidden * hidden, axis=1, keepdims=True)) + EPSILON)
    normed = (hidden * scale_row * norm_gain.astype(jnp.float32)[None, :]).astype(jnp.bfloat16)
    queries = jnp.dot(normed, w_query, preferred_element_type=jnp.float32).reshape(NEW, HQ, HD)
    queries = lax.optimization_barrier(rotate(queries, places).astype(jnp.bfloat16))
    new_keys = jnp.dot(normed, w_key, preferred_element_type=jnp.float32).reshape(NEW, KVH, HD)
    new_keys = lax.optimization_barrier(rotate(new_keys, places).astype(jnp.bfloat16))
    new_values = lax.optimization_barrier(jnp.dot(normed, w_value, preferred_element_type=jnp.float32).astype(jnp.bfloat16))
    new_k32 = new_keys.astype(jnp.float32)
    new_v32 = new_values.reshape(NEW, KVH, HD).astype(jnp.float32)
    owner = jnp.argsort(block_of_shard).astype(jnp.int32)
    padding = jnp.zeros((MAXLEN, KVH, HD), jnp.float32)
    packed_keys = cache_keys.reshape(N_SEQ, CACHE_DEV, KVH * HD)[owner].reshape(CACHE_ROWS, KVH, HD).astype(jnp.float32)
    packed_keys = jnp.concatenate([packed_keys, padding], axis=0)
    packed_values = cache_values.reshape(N_SEQ, CACHE_DEV, KVH * HD)[owner].reshape(CACHE_ROWS, KVH, HD).astype(jnp.float32)
    packed_values = jnp.concatenate([packed_values, padding], axis=0)
    starts = (jnp.cumsum(cached_len) - cached_len).astype(jnp.int32)
    groups = HQ // KVH

    def attend(block_item):
        q_block, req_one, pos_block = block_item
        begin = jnp.take(starts, req_one)
        length = jnp.take(cached_len, req_one)
        cache_k = lax.dynamic_slice_in_dim(packed_keys, begin, MAXLEN, 0)
        cache_v = lax.dynamic_slice_in_dim(packed_values, begin, MAXLEN, 0)
        rows_here = q_block.shape[0]
        q_four = q_block.astype(jnp.float32).reshape(rows_here, KVH, groups, HD)
        cache_scores = jnp.einsum('bcgd,kcd->bcgk', q_four, cache_k) * HD ** (-0.5)
        new_scores = jnp.einsum('bcgd,kcd->bcgk', q_four, new_k32) * HD ** (-0.5)
        cache_ok = jnp.broadcast_to((jnp.arange(MAXLEN, dtype=jnp.int32) < length)[None, :], (rows_here, MAXLEN))
        new_ok = (request[None, :] == req_one) & (places[None, :] <= pos_block[:, None])
        visible = jnp.concatenate([cache_ok, new_ok], axis=1)[:, None, None, :]
        scores = jnp.where(visible, jnp.concatenate([cache_scores, new_scores], axis=-1), NEGATIVE)
        row_top = lax.optimization_barrier(jnp.max(scores, axis=-1))
        weights = jnp.where(visible, jnp.exp(scores - row_top[..., None]), 0.0)
        denominator = lax.optimization_barrier(jnp.sum(weights, axis=-1))
        rounded = lax.optimization_barrier(weights.astype(jnp.bfloat16)).astype(jnp.float32)
        numerator = jnp.einsum('bcgk,kcd->bcgd', rounded[..., :MAXLEN], cache_v)
        numerator = numerator + jnp.einsum('bcgk,kcd->bcgd', rounded[..., MAXLEN:], new_v32)
        return (numerator / denominator[..., None]).astype(jnp.bfloat16).reshape(rows_here, HQ * HD)
    boundary = PREFILLS * SPAN
    sub_rows = min(SPAN, 128)
    pieces = SPAN // sub_rows
    flat_q = queries.reshape(NEW, HQ * HD)
    prefill_q = flat_q[:boundary].reshape(PREFILLS * pieces, sub_rows, HQ * HD)
    prefill_places = places[:boundary].reshape(PREFILLS * pieces, sub_rows)
    prefill_request = jnp.repeat(jnp.arange(PREFILLS, dtype=jnp.int32), pieces).astype(jnp.int32)
    prefill_out = lax.map(attend, (prefill_q, prefill_request, prefill_places))
    decode_q = flat_q[boundary:].reshape(DECODES, 1, HQ * HD)
    decode_places = places[boundary:].reshape(DECODES, 1)
    decode_request = (PREFILLS + jnp.arange(DECODES, dtype=jnp.int32)).astype(jnp.int32)
    decode_out = lax.map(attend, (decode_q, decode_request, decode_places))
    attended = jnp.concatenate([prefill_out.reshape(boundary, HQ * HD), decode_out.reshape(DECODES, HQ * HD)], axis=0)
    return jnp.dot(attended, w_out, preferred_element_type=jnp.float32).astype(jnp.bfloat16)
```

```python
import functools

import jax
import jax.numpy as jnp
from jax import lax
from jax.experimental import pallas as pl
from jax.experimental.pallas import tpu as pltpu
from jax.sharding import PartitionSpec as P

HD = 128
SPAN = 512
PREFILLS = 2
TILE = 256
NEGATIVE = -1e30
THETA = 1000000.0
EPSILON = 1e-06
SCALE = HD ** (-0.5)


def rotate(values, places):
    half_dim = values.shape[-1] // 2
    frequency = THETA ** (-jnp.arange(half_dim, dtype=jnp.float32) / half_dim)
    angles = places.astype(jnp.float32)[:, None] * frequency[None, :]
    cosine = jnp.cos(angles)[:, None, :]
    sine_part = jnp.sin(angles)[:, None, :]
    front_half = values[..., :half_dim]
    second = values[..., half_dim:]
    return jnp.concatenate(
        [front_half * cosine - second * sine_part, second * cosine + front_half * sine_part],
        axis=-1,
    )


def nt_dot(a, b):
    return lax.dot_general(a, b, (((1,), (1,)), ((), ())), preferred_element_type=jnp.float32)


def tn_dot(a, b):
    return lax.dot_general(a, b, (((0,), (0,)), ((), ())), preferred_element_type=jnp.float32)


def tile_step(q, k, v, lo, hi, first, state, top_ref, sum_ref, acc_ref, width):
    scores = nt_dot(k, q) * SCALE
    index = first + lax.broadcasted_iota(jnp.int32, scores.shape, 0)
    visible = (index >= lo) & (index < hi)
    scores = jnp.where(visible, scores, NEGATIVE)
    old = top_ref[:, :width]
    top = jnp.maximum(old, jnp.max(scores, axis=0, keepdims=True))
    weights = jnp.where(visible, jnp.exp(scores - top), 0.0)
    factor = jnp.exp(old - top)
    top_ref[:, :width] = top
    sum_ref[:, :width] = sum_ref[:, :width] * factor + jnp.sum(weights, axis=0, keepdims=True)
    acc_ref[:, :width] = acc_ref[:, :width] * factor + tn_dot(v, weights.astype(jnp.bfloat16))


def begin(top_ref, sum_ref, acc_ref):
    top_ref[...] = jnp.full(top_ref.shape, NEGATIVE, jnp.float32)
    sum_ref[...] = jnp.zeros(sum_ref.shape, jnp.float32)
    acc_ref[...] = jnp.zeros(acc_ref.shape, jnp.float32)


def finish(top_ref, sum_ref, acc_ref, width):
    total = sum_ref[:, :width]
    some = total > 0.0
    safe = jnp.where(some, total, 1.0)
    out = acc_ref[:, :width] / safe
    return out, jnp.where(some, top_ref[:, :width] + jnp.log(safe), NEGATIVE)


def cache_kernel(range_ref, lo_ref, hi_ref, q_ref, k_ref, v_ref, o_ref, l_ref, top_ref, sum_ref, acc_ref):
    groups = q_ref.shape[1] // HD
    boundary = PREFILLS * SPAN
    decodes = q_ref.shape[0] - boundary
    tiles = k_ref.shape[0] // TILE

    def attend(q, lo, hi, first_tile, last_tile, width):
        begin(top_ref, sum_ref, acc_ref)

        @pl.loop(first_tile, last_tile)
        def _(tile):
            first = pl.multiple_of(tile * TILE, TILE)
            tile_step(
                q, k_ref[pl.ds(first, TILE), :], v_ref[pl.ds(first, TILE), :],
                lo, hi, first, None, top_ref, sum_ref, acc_ref, width,
            )

        return finish(top_ref, sum_ref, acc_ref, width)

    q = jnp.concatenate(
        [q_ref[boundary:, g * HD:(g + 1) * HD] for g in range(groups)], axis=0
    )
    out, lse = attend(q, lo_ref[...], hi_ref[...], 0, tiles, groups * decodes)
    out = out.T.astype(jnp.bfloat16)
    for g in range(groups):
        o_ref[boundary:, g * HD:(g + 1) * HD] = out[g * decodes:(g + 1) * decodes]
        l_ref[0, g:g + 1, boundary:] = lse[:, g * decodes:(g + 1) * decodes]
    for r in range(PREFILLS):
        lo, hi = range_ref[2 * r], range_ref[2 * r + 1]
        rows = slice(r * SPAN, (r + 1) * SPAN)

        @pl.when(hi > lo)
        def _():
            for g in range(groups):
                q = q_ref[rows, g * HD:(g + 1) * HD]
                out, lse = attend(q, lo, hi, lo // TILE, (hi + TILE - 1) // TILE, SPAN)
                o_ref[rows, g * HD:(g + 1) * HD] = out.T.astype(jnp.bfloat16)
                l_ref[0, g:g + 1, rows] = lse

        @pl.when(hi <= lo)
        def _():
            o_ref[rows, :] = jnp.zeros((SPAN, groups * HD), jnp.bfloat16)
            l_ref[0, :, rows] = jnp.full((groups, SPAN), NEGATIVE, jnp.float32)


def cache_attention(ranges, lo, hi, queries, keys, values):
    rows, q_width = queries.shape
    slots, kv_width = keys.shape
    kv_heads = kv_width // HD
    groups = q_width // kv_width
    whole = lambda c: (0, 0)
    column = lambda c: (0, c)
    return pl.pallas_call(
        cache_kernel,
        name="cache_attention",
        grid=(kv_heads,),
        out_shape=(
            jax.ShapeDtypeStruct((rows, q_width), jnp.bfloat16),
            jax.ShapeDtypeStruct((kv_heads, groups, rows), jnp.float32),
        ),
        in_specs=[
            pl.BlockSpec(memory_space=pltpu.SMEM),
            pl.BlockSpec(lo.shape, whole),
            pl.BlockSpec(hi.shape, whole),
            pl.BlockSpec((rows, groups * HD), column),
            pl.BlockSpec((slots, HD), column),
            pl.BlockSpec((slots, HD), column),
        ],
        out_specs=(
            pl.BlockSpec((rows, groups * HD), column),
            pl.BlockSpec((1, groups, rows), lambda c: (c, 0, 0)),
        ),
        scratch_shapes=[
            pltpu.VMEM((1, SPAN), jnp.float32),
            pltpu.VMEM((1, SPAN), jnp.float32),
            pltpu.VMEM((HD, SPAN), jnp.float32),
        ],
        compiler_params=pltpu.CompilerParams(vmem_limit_bytes=32 << 20),
        cost_estimate=pl.CostEstimate(
            flops=4 * slots * q_width * 512, bytes_accessed=8 << 20, transcendentals=1 << 20
        ),
    )(ranges, lo, hi, queries, keys, values)


def self_kernel(lo_ref, hi_ref, q_ref, k_ref, v_ref, o_ref, l_ref):
    groups = q_ref.shape[1] // HD
    keys, values = k_ref[...], v_ref[...]
    for g in range(groups):
        scores = nt_dot(keys, q_ref[:, g * HD:(g + 1) * HD]) * SCALE
        index = lax.broadcasted_iota(jnp.int32, scores.shape, 0)
        visible = (index >= lo_ref[...]) & (index <= hi_ref[...])
        scores = jnp.where(visible, scores, NEGATIVE)
        top = jnp.max(scores, axis=0, keepdims=True)
        weights = jnp.where(visible, jnp.exp(scores - top), 0.0)
        total = jnp.sum(weights, axis=0, keepdims=True)
        out = tn_dot(values, weights.astype(jnp.bfloat16)) / total
        o_ref[:, g * HD:(g + 1) * HD] = out.T
        l_ref[0, g:g + 1, :] = top + jnp.log(total)


def self_attention(lo, hi, queries, new):
    rows, q_width = queries.shape
    count, width = new.shape
    kv_heads = width // (2 * HD)
    groups = q_width // HD // kv_heads
    return pl.pallas_call(
        self_kernel,
        name="new_row_attention",
        grid=(kv_heads,),
        out_shape=(
            jax.ShapeDtypeStruct((rows, q_width), jnp.float32),
            jax.ShapeDtypeStruct((kv_heads, groups, rows), jnp.float32),
        ),
        in_specs=[
            pl.BlockSpec(lo.shape, lambda c: (0, 0)),
            pl.BlockSpec(hi.shape, lambda c: (0, 0)),
            pl.BlockSpec((rows, groups * HD), lambda c: (0, c)),
            pl.BlockSpec((count, HD), lambda c: (0, c)),
            pl.BlockSpec((count, HD), lambda c: (0, kv_heads + c)),
        ],
        out_specs=(
            pl.BlockSpec((rows, groups * HD), lambda c: (0, c)),
            pl.BlockSpec((1, groups, rows), lambda c: (c, 0, 0)),
        ),
        compiler_params=pltpu.CompilerParams(vmem_limit_bytes=32 << 20),
        cost_estimate=pl.CostEstimate(
            flops=4 * count * q_width * rows, bytes_accessed=4 << 20, transcendentals=1 << 20
        ),
    )(lo, hi, queries, new, new)


def per_device(
    tokens,
    norm_gain,
    w_query,
    w_key,
    w_value,
    w_out,
    cache_keys,
    cache_values,
    cached_len,
    block_of_shard,
):
    seq_count = lax.axis_size("seq")
    seq_index = lax.axis_index("seq")
    tok_rows = tokens.shape[0]
    all_rows = tok_rows * seq_count
    q_heads = w_query.shape[1] // HD
    kv_heads = w_key.shape[1] // HD
    groups = q_heads // kv_heads
    slots = cache_keys.shape[0]
    requests = cached_len.shape[0]
    boundary = PREFILLS * SPAN

    number = jnp.arange(requests, dtype=jnp.int32)
    ends = jnp.sum(jnp.where(number[None, :] <= number[:, None], cached_len[None, :], 0), axis=1)
    base = block_of_shard[0] * slots
    lows = jnp.clip(ends - cached_len - base, 0, slots)
    highs = jnp.clip(ends - base, 0, slots)
    ranges = jnp.stack([lows[:PREFILLS], highs[:PREFILLS]], axis=1).reshape(-1)
    decode_lo = jnp.tile(lows[PREFILLS:], groups)[None, :]
    decode_hi = jnp.tile(highs[PREFILLS:], groups)[None, :]

    my_rows = seq_index * tok_rows + jnp.arange(tok_rows, dtype=jnp.int32)
    prefill = my_rows < boundary
    my_request = jnp.where(prefill, my_rows // SPAN, PREFILLS + my_rows - boundary)
    my_begin = jnp.sum(
        jnp.where(my_request[:, None] == number[None, :], cached_len[None, :], 0), axis=1
    )
    my_position = my_begin + jnp.where(prefill, my_rows % SPAN, 0)

    hidden = tokens.astype(jnp.float32)
    scale_row = lax.rsqrt(jnp.mean(hidden * hidden, axis=1, keepdims=True) + EPSILON)
    normed = (hidden * scale_row * norm_gain.astype(jnp.float32)[None, :]).astype(jnp.bfloat16)
    queries = jnp.dot(normed, w_query, preferred_element_type=jnp.float32).reshape(
        tok_rows, q_heads, HD
    )
    queries = rotate(queries, my_position).astype(jnp.bfloat16).reshape(tok_rows, q_heads * HD)
    new_keys = jnp.dot(normed, w_key, preferred_element_type=jnp.float32).reshape(
        tok_rows, kv_heads, HD
    )
    new_keys = rotate(new_keys, my_position).astype(jnp.bfloat16).reshape(tok_rows, kv_heads * HD)
    new_values = jnp.dot(normed, w_value, preferred_element_type=jnp.float32).astype(jnp.bfloat16)
    gathered = lax.all_gather(queries, "seq", axis=0, tiled=True)
    new = lax.all_gather(
        jnp.concatenate([new_keys, new_values], axis=1), "seq", axis=0, tiled=True
    )

    part, part_lse = cache_attention(
        ranges, decode_lo, decode_hi, gathered, cache_keys, cache_values
    )
    part_lse = part_lse.reshape(q_heads, all_rows)
    every_lse = lax.all_gather(part_lse, "seq", axis=0)
    most = jnp.max(every_lse, axis=0)
    cache_lse = most + jnp.log(jnp.sum(jnp.exp(every_lse - most[None]), axis=0))
    share = jnp.where(part_lse > 0.5 * NEGATIVE, jnp.exp(part_lse - cache_lse), 0.0)
    part = part.reshape(all_rows, q_heads, HD).astype(jnp.float32) * share.T[:, :, None]
    part = part.astype(jnp.bfloat16).reshape(seq_count, tok_rows, q_heads * HD)
    cached = lax.psum_scatter(part, "seq", scatter_dimension=0)

    padded = -(-tok_rows // 128) * 128
    lane_rows = seq_index * tok_rows + jnp.minimum(
        jnp.arange(padded, dtype=jnp.int32), tok_rows - 1
    )
    first_key = jnp.where(lane_rows < boundary, lane_rows // SPAN * SPAN, lane_rows)
    own, own_lse = self_attention(
        first_key[None, :],
        lane_rows[None, :],
        jnp.pad(queries, ((0, padded - tok_rows), (0, 0))),
        new,
    )
    own = own[:tok_rows].reshape(tok_rows, q_heads, HD)
    own_lse = own_lse.reshape(q_heads, padded)[:, :tok_rows]
    my_cache_lse = lax.dynamic_slice_in_dim(cache_lse, seq_index * tok_rows, tok_rows, axis=1)
    top = jnp.maximum(own_lse, my_cache_lse)
    own_weight = jnp.exp(own_lse - top)
    cache_weight = jnp.exp(my_cache_lse - top)
    norm = own_weight + cache_weight
    own_weight = (own_weight / norm).T[:, :, None]
    cache_weight = (cache_weight / norm).T[:, :, None]
    cached = cached.reshape(tok_rows, q_heads, HD).astype(jnp.float32)
    attended = (own * own_weight + cached * cache_weight).astype(jnp.bfloat16)
    attended = attended.reshape(tok_rows, q_heads * HD)
    partial_out = jnp.dot(attended, w_out, preferred_element_type=jnp.float32)
    return lax.psum_scatter(partial_out.astype(jnp.bfloat16), "tp", scatter_dimension=1, tiled=True)


def solution(mesh):
    in_specs = (
        P("seq", None),
        P(),
        P(None, "tp"),
        P(None, "tp"),
        P(None, "tp"),
        P("tp", None),
        P("seq", "tp"),
        P("seq", "tp"),
        P(),
        P("seq"),
    )
    out_specs = P("seq", "tp")
    return jax.shard_map(
        per_device, mesh=mesh, in_specs=in_specs, out_specs=out_specs, check_vma=False
    )
```

```python
import functools

import jax
import jax.numpy as jnp
from jax import lax
from jax.experimental import pallas as pl
from jax.experimental.pallas import tpu as pltpu
from jax.sharding import PartitionSpec as P

HD = 128
SPAN = 512
PREFILLS = 2
TILE = 256
NEGATIVE = -1e30
THETA = 1000000.0
EPSILON = 1e-06
SCALE = HD ** (-0.5)


def rotate(values, places):
    half_dim = values.shape[-1] // 2
    frequency = THETA ** (-jnp.arange(half_dim, dtype=jnp.float32) / half_dim)
    angles = places.astype(jnp.float32)[:, None] * frequency[None, :]
    cosine = jnp.cos(angles)[:, None, :]
    sine_part = jnp.sin(angles)[:, None, :]
    front_half = values[..., :half_dim]
    second = values[..., half_dim:]
    return jnp.concatenate(
        [front_half * cosine - second * sine_part, second * cosine + front_half * sine_part],
        axis=-1,
    )


def nt_dot(a, b):
    return lax.dot_general(a, b, (((1,), (1,)), ((), ())), preferred_element_type=jnp.float32)


def tn_dot(a, b):
    return lax.dot_general(a, b, (((0,), (0,)), ((), ())), preferred_element_type=jnp.float32)


def tile_step(q, k, v, lo, hi, first, state, top_ref, sum_ref, acc_ref, width):
    scores = nt_dot(k, q) * SCALE
    index = first + lax.broadcasted_iota(jnp.int32, scores.shape, 0)
    visible = (index >= lo) & (index < hi)
    scores = jnp.where(visible, scores, NEGATIVE)
    old = top_ref[:, :width]
    top = jnp.maximum(old, jnp.max(scores, axis=0, keepdims=True))
    weights = jnp.where(visible, jnp.exp(scores - top), 0.0)
    factor = jnp.exp(old - top)
    top_ref[:, :width] = top
    sum_ref[:, :width] = sum_ref[:, :width] * factor + jnp.sum(weights, axis=0, keepdims=True)
    acc_ref[:, :width] = acc_ref[:, :width] * factor + tn_dot(v, weights.astype(jnp.bfloat16))


def begin(top_ref, sum_ref, acc_ref):
    top_ref[...] = jnp.full(top_ref.shape, NEGATIVE, jnp.float32)
    sum_ref[...] = jnp.zeros(sum_ref.shape, jnp.float32)
    acc_ref[...] = jnp.zeros(acc_ref.shape, jnp.float32)


def finish(top_ref, sum_ref, acc_ref, width):
    total = sum_ref[:, :width]
    some = total > 0.0
    safe = jnp.where(some, total, 1.0)
    out = acc_ref[:, :width] / safe
    return out, jnp.where(some, top_ref[:, :width] + jnp.log(safe), NEGATIVE)


def cache_kernel(range_ref, lo_ref, hi_ref, q_ref, k_ref, v_ref, o_ref, l_ref, top_ref, sum_ref, acc_ref):
    groups = q_ref.shape[1] // HD
    boundary = PREFILLS * SPAN
    decodes = q_ref.shape[0] - boundary

    def attend(q, lo, hi, first_tile, last_tile, width):
        begin(top_ref, sum_ref, acc_ref)

        @pl.loop(first_tile, last_tile)
        def _(tile):
            first = pl.multiple_of(tile * TILE, TILE)
            tile_step(
                q, k_ref[pl.ds(first, TILE), :], v_ref[pl.ds(first, TILE), :],
                lo, hi, first, None, top_ref, sum_ref, acc_ref, width,
            )

        return finish(top_ref, sum_ref, acc_ref, width)

    q = jnp.concatenate(
        [q_ref[boundary:, g * HD:(g + 1) * HD] for g in range(groups)], axis=0
    )
    scores = nt_dot(k_ref[...], q) * SCALE
    index = lax.broadcasted_iota(jnp.int32, scores.shape, 0)
    visible = (index >= lo_ref[...]) & (index < hi_ref[...])
    scores = jnp.where(visible, scores, NEGATIVE)
    top = jnp.max(scores, axis=0, keepdims=True)
    weights = jnp.where(visible, jnp.exp(scores - top), 0.0)
    total = jnp.sum(weights, axis=0, keepdims=True)
    some = total > 0.0
    safe = jnp.where(some, total, 1.0)
    out = tn_dot(v_ref[...], weights.astype(jnp.bfloat16)) / safe
    lse = jnp.where(some, top + jnp.log(safe), NEGATIVE)
    out = out.T.astype(jnp.bfloat16)
    for g in range(groups):
        o_ref[boundary:, g * HD:(g + 1) * HD] = out[g * decodes:(g + 1) * decodes]
        l_ref[0, g:g + 1, boundary:] = lse[:, g * decodes:(g + 1) * decodes]
    for r in range(PREFILLS):
        lo, hi = range_ref[2 * r], range_ref[2 * r + 1]
        rows = slice(r * SPAN, (r + 1) * SPAN)

        @pl.when(hi > lo)
        def _():
            for g in range(groups):
                q = q_ref[rows, g * HD:(g + 1) * HD]
                out, lse = attend(q, lo, hi, lo // TILE, (hi + TILE - 1) // TILE, SPAN)
                o_ref[rows, g * HD:(g + 1) * HD] = out.T.astype(jnp.bfloat16)
                l_ref[0, g:g + 1, rows] = lse

        @pl.when(hi <= lo)
        def _():
            o_ref[rows, :] = jnp.zeros((SPAN, groups * HD), jnp.bfloat16)
            l_ref[0, :, rows] = jnp.full((groups, SPAN), NEGATIVE, jnp.float32)


def cache_attention(ranges, lo, hi, queries, keys, values):
    rows, q_width = queries.shape
    slots, kv_width = keys.shape
    kv_heads = kv_width // HD
    groups = q_width // kv_width
    whole = lambda c: (0, 0)
    column = lambda c: (0, c)
    return pl.pallas_call(
        cache_kernel,
        name="cache_attention",
        grid=(kv_heads,),
        out_shape=(
            jax.ShapeDtypeStruct((rows, q_width), jnp.bfloat16),
            jax.ShapeDtypeStruct((kv_heads, groups, rows), jnp.float32),
        ),
        in_specs=[
            pl.BlockSpec(memory_space=pltpu.SMEM),
            pl.BlockSpec(lo.shape, whole),
            pl.BlockSpec(hi.shape, whole),
            pl.BlockSpec((rows, groups * HD), column),
            pl.BlockSpec((slots, HD), column),
            pl.BlockSpec((slots, HD), column),
        ],
        out_specs=(
            pl.BlockSpec((rows, groups * HD), column),
            pl.BlockSpec((1, groups, rows), lambda c: (c, 0, 0)),
        ),
        scratch_shapes=[
            pltpu.VMEM((1, SPAN), jnp.float32),
            pltpu.VMEM((1, SPAN), jnp.float32),
            pltpu.VMEM((HD, SPAN), jnp.float32),
        ],
        compiler_params=pltpu.CompilerParams(vmem_limit_bytes=32 << 20),
        cost_estimate=pl.CostEstimate(
            flops=4 * slots * q_width * 512, bytes_accessed=8 << 20, transcendentals=1 << 20
        ),
    )(ranges, lo, hi, queries, keys, values)


def self_kernel(lo_ref, hi_ref, q_ref, k_ref, v_ref, o_ref, l_ref):
    groups = q_ref.shape[1] // HD
    keys, values = k_ref[...], v_ref[...]
    for g in range(groups):
        scores = nt_dot(keys, q_ref[:, g * HD:(g + 1) * HD]) * SCALE
        index = lax.broadcasted_iota(jnp.int32, scores.shape, 0)
        visible = (index >= lo_ref[...]) & (index <= hi_ref[...])
        scores = jnp.where(visible, scores, NEGATIVE)
        top = jnp.max(scores, axis=0, keepdims=True)
        weights = jnp.where(visible, jnp.exp(scores - top), 0.0)
        total = jnp.sum(weights, axis=0, keepdims=True)
        out = tn_dot(values, weights.astype(jnp.bfloat16)) / total
        o_ref[:, g * HD:(g + 1) * HD] = out.T
        l_ref[0, g:g + 1, :] = top + jnp.log(total)


def self_attention(lo, hi, queries, new):
    rows, q_width = queries.shape
    count, width = new.shape
    kv_heads = width // (2 * HD)
    groups = q_width // HD // kv_heads
    return pl.pallas_call(
        self_kernel,
        name="new_row_attention",
        grid=(kv_heads,),
        out_shape=(
            jax.ShapeDtypeStruct((rows, q_width), jnp.float32),
            jax.ShapeDtypeStruct((kv_heads, groups, rows), jnp.float32),
        ),
        in_specs=[
            pl.BlockSpec(lo.shape, lambda c: (0, 0)),
            pl.BlockSpec(hi.shape, lambda c: (0, 0)),
            pl.BlockSpec((rows, groups * HD), lambda c: (0, c)),
            pl.BlockSpec((count, HD), lambda c: (0, c)),
            pl.BlockSpec((count, HD), lambda c: (0, kv_heads + c)),
        ],
        out_specs=(
            pl.BlockSpec((rows, groups * HD), lambda c: (0, c)),
            pl.BlockSpec((1, groups, rows), lambda c: (c, 0, 0)),
        ),
        compiler_params=pltpu.CompilerParams(vmem_limit_bytes=32 << 20),
        cost_estimate=pl.CostEstimate(
            flops=4 * count * q_width * rows, bytes_accessed=4 << 20, transcendentals=1 << 20
        ),
    )(lo, hi, queries, new, new)


def flip(index, bit):
    return index + bit - 2 * bit * ((index // bit) % 2)


def greet(peers):
    barrier = pltpu.get_barrier_semaphore()
    for peer in peers:
        pl.semaphore_signal(
            barrier,
            inc=1,
            device_id=(peer, lax.axis_index("tp")),
            device_id_type=pl.DeviceIdType.MESH,
        )
    pl.semaphore_wait(barrier, len(peers))


def offset_index(index, offset, bits):
    for bit in bits:
        if offset & bit:
            index = flip(index, bit)
    return index


def gather_kernel(bits, x_ref, out_ref, own_sem, send_sem, recv_sem):
    me = lax.axis_index("seq")
    greet([flip(me, bit) for bit in bits])
    half = x_ref.shape[1] // 2
    orders = [list(bits), list(bits[:-2]) + [bits[-1], bits[-2]]]
    own = pltpu.make_async_copy(x_ref, out_ref.at[me], own_sem)
    own.start()
    held = [[0], [0]]
    sends, got, number = [], {}, [0, 0]
    for step in range(len(bits)):
        fresh = [[], []]
        for place in range(len(held[0])):
            for part in range(2):
                bit, offset = orders[part][step], held[part][place]
                columns = pl.ds(part * half, half)
                if offset and (part, offset) in got:
                    got.pop((part, offset)).wait_recv()
                block = offset_index(me, offset, bits)
                copy = pltpu.make_async_remote_copy(
                    src_ref=out_ref.at[block, :, columns] if offset else x_ref.at[:, columns],
                    dst_ref=out_ref.at[block, :, columns],
                    send_sem=send_sem.at[part, number[part]],
                    recv_sem=recv_sem.at[part, offset ^ bit],
                    device_id=(flip(me, bit), lax.axis_index("tp")),
                    device_id_type=pl.DeviceIdType.MESH,
                )
                copy.start()
                number[part] += 1
                sends.append(copy)
                fresh[part].append((offset ^ bit, copy))
        for part in range(2):
            for offset, copy in fresh[part]:
                held[part].append(offset)
                got[(part, offset)] = copy
    for copy in got.values():
        copy.wait_recv()
    for copy in sends:
        copy.wait_send()
    own.wait()


def gather(block, count):
    bits = []
    while 1 << len(bits) < count:
        bits.insert(0, 1 << len(bits))
    return pl.pallas_call(
        functools.partial(gather_kernel, bits),
        name="gather_rows",
        out_shape=jax.ShapeDtypeStruct((count,) + block.shape, block.dtype),
        in_specs=[pl.BlockSpec(memory_space=pl.ANY)],
        out_specs=pl.BlockSpec(memory_space=pl.ANY),
        scratch_shapes=[
            pltpu.SemaphoreType.DMA,
            pltpu.SemaphoreType.DMA((2, count - 1)),
            pltpu.SemaphoreType.DMA((2, count)),
        ],
        compiler_params=pltpu.CompilerParams(collective_id=0, has_side_effects=True),
        cost_estimate=pl.CostEstimate(
            flops=0, bytes_accessed=100 << 20, transcendentals=0
        ),
    )(block)


def exchange_kernel(count, x_ref, l_ref, out_ref, lout_ref, own_sem, send_sem, recv_sem):
    me = lax.axis_index("seq")
    peers = [lax.rem(me + k, count) for k in range(1, count)]
    greet(peers)
    own = pltpu.make_async_copy(x_ref.at[me], out_ref.at[me], own_sem.at[0])
    own_lse = pltpu.make_async_copy(l_ref.at[me], lout_ref.at[me], own_sem.at[1])
    own.start()
    own_lse.start()
    copies = []
    for k in range(1, count):
        for part, (source, target) in enumerate(((x_ref, out_ref), (l_ref, lout_ref))):
            copy = pltpu.make_async_remote_copy(
                src_ref=source.at[peers[k - 1]],
                dst_ref=target.at[me],
                send_sem=send_sem.at[part, k],
                recv_sem=recv_sem.at[part, k],
                device_id=(peers[k - 1], lax.axis_index("tp")),
                device_id_type=pl.DeviceIdType.MESH,
            )
            copy.start()
            copies.append((part, k, copy))
    for part, k, copy in copies:
        copy.wait_send()
        copy.wait_recv()
    own.wait()
    own_lse.wait()


def exchange(blocks, lse):
    count = blocks.shape[0]
    any_spec = pl.BlockSpec(memory_space=pl.ANY)
    return pl.pallas_call(
        functools.partial(exchange_kernel, count),
        name="exchange_partials",
        out_shape=(
            jax.ShapeDtypeStruct(blocks.shape, blocks.dtype),
            jax.ShapeDtypeStruct(lse.shape, lse.dtype),
        ),
        in_specs=[any_spec, any_spec],
        out_specs=(any_spec, any_spec),
        scratch_shapes=[
            pltpu.SemaphoreType.DMA((2,)),
            pltpu.SemaphoreType.DMA((2, count)),
            pltpu.SemaphoreType.DMA((2, count)),
        ],
        compiler_params=pltpu.CompilerParams(collective_id=1, has_side_effects=True),
        cost_estimate=pl.CostEstimate(
            flops=0, bytes_accessed=160 << 20, transcendentals=0
        ),
    )(blocks, lse)


def flat_blocks(values, count, flat):
    values = values.reshape(count, -1, HD)
    return jnp.pad(values, ((0, 0), (0, flat - values.shape[1]), (0, 0)))


def per_device(
    tokens,
    norm_gain,
    w_query,
    w_key,
    w_value,
    w_out,
    cache_keys,
    cache_values,
    cached_len,
    block_of_shard,
):
    seq_count = lax.axis_size("seq")
    seq_index = lax.axis_index("seq")
    tok_rows = tokens.shape[0]
    all_rows = tok_rows * seq_count
    q_heads = w_query.shape[1] // HD
    kv_heads = w_key.shape[1] // HD
    groups = q_heads // kv_heads
    slots = cache_keys.shape[0]
    requests = cached_len.shape[0]
    boundary = PREFILLS * SPAN

    number = jnp.arange(requests, dtype=jnp.int32)
    ends = jnp.sum(jnp.where(number[None, :] <= number[:, None], cached_len[None, :], 0), axis=1)
    base = block_of_shard[0] * slots
    lows = jnp.clip(ends - cached_len - base, 0, slots)
    highs = jnp.clip(ends - base, 0, slots)
    ranges = jnp.stack([lows[:PREFILLS], highs[:PREFILLS]], axis=1).reshape(-1)
    decode_lo = jnp.tile(lows[PREFILLS:], groups)[None, :]
    decode_hi = jnp.tile(highs[PREFILLS:], groups)[None, :]

    my_rows = seq_index * tok_rows + jnp.arange(tok_rows, dtype=jnp.int32)
    prefill = my_rows < boundary
    my_request = jnp.where(prefill, my_rows // SPAN, PREFILLS + my_rows - boundary)
    my_begin = jnp.sum(
        jnp.where(my_request[:, None] == number[None, :], cached_len[None, :], 0), axis=1
    )
    my_position = my_begin + jnp.where(prefill, my_rows % SPAN, 0)

    hidden = tokens.astype(jnp.float32)
    scale_row = lax.rsqrt(jnp.mean(hidden * hidden, axis=1, keepdims=True) + EPSILON)
    normed = (hidden * scale_row * norm_gain.astype(jnp.float32)[None, :]).astype(jnp.bfloat16)
    queries = jnp.dot(normed, w_query, preferred_element_type=jnp.float32).reshape(
        tok_rows, q_heads, HD
    )
    queries = rotate(queries, my_position).astype(jnp.bfloat16).reshape(tok_rows, q_heads * HD)
    new_keys = jnp.dot(normed, w_key, preferred_element_type=jnp.float32).reshape(
        tok_rows, kv_heads, HD
    )
    new_keys = rotate(new_keys, my_position).astype(jnp.bfloat16).reshape(tok_rows, kv_heads * HD)
    new_values = jnp.dot(normed, w_value, preferred_element_type=jnp.float32).astype(jnp.bfloat16)
    lines = tok_rows * q_heads
    flat = -(-lines // 16) * 16
    gathered = gather(
        jnp.pad(queries, ((0, -(-tok_rows // 16) * 16 - tok_rows), (0, 0))), seq_count
    )
    gathered = gathered[:, :tok_rows].reshape(all_rows, q_heads * HD)
    new = lax.all_gather(
        jnp.concatenate([new_keys, new_values], axis=1), "seq", axis=0, tiled=True
    )

    part, part_lse = cache_attention(
        ranges, decode_lo, decode_hi, gathered, cache_keys, cache_values
    )
    part_lse = part_lse.reshape(q_heads, seq_count, tok_rows).transpose(1, 0, 2)
    lanes = -(-tok_rows // 128) * 128
    head_rows = -(-q_heads // 8) * 8
    part_lse = jnp.pad(
        part_lse, ((0, 0), (0, head_rows - q_heads), (0, lanes - tok_rows))
    )
    parts, parts_lse = exchange(flat_blocks(part, seq_count, flat), part_lse)
    parts = parts[:, :lines].reshape(seq_count, tok_rows, q_heads, HD)
    parts_lse = parts_lse[:, :q_heads, :tok_rows].transpose(0, 2, 1)

    padded = -(-tok_rows // 128) * 128
    lane_rows = seq_index * tok_rows + jnp.minimum(
        jnp.arange(padded, dtype=jnp.int32), tok_rows - 1
    )
    first_key = jnp.where(lane_rows < boundary, lane_rows // SPAN * SPAN, lane_rows)
    own, own_lse = self_attention(
        first_key[None, :],
        lane_rows[None, :],
        jnp.pad(queries, ((0, padded - tok_rows), (0, 0))),
        new,
    )
    own = own[:tok_rows].reshape(tok_rows, q_heads, HD)
    own_lse = own_lse.reshape(q_heads, padded)[:, :tok_rows].T
    top = jnp.maximum(own_lse, jnp.max(parts_lse, axis=0))
    own_weight = jnp.exp(own_lse - top)
    weights = jnp.exp(parts_lse - top[None])
    norm = own_weight + jnp.sum(weights, axis=0)
    cached = jnp.sum(parts.astype(jnp.float32) * weights[..., None], axis=0)
    attended = (own * own_weight[..., None] + cached) / norm[..., None]
    attended = attended.astype(jnp.bfloat16)
    attended = attended.reshape(tok_rows, q_heads * HD)
    partial_out = jnp.dot(attended, w_out, preferred_element_type=jnp.float32)
    return lax.psum_scatter(partial_out.astype(jnp.bfloat16), "tp", scatter_dimension=1, tiled=True)


def solution(mesh):
    in_specs = (
        P("seq", None),
        P(),
        P(None, "tp"),
        P(None, "tp"),
        P(None, "tp"),
        P("tp", None),
        P("seq", "tp"),
        P("seq", "tp"),
        P(),
        P("seq"),
    )
    out_specs = P("seq", "tp")
    return jax.shard_map(
        per_device, mesh=mesh, in_specs=in_specs, out_specs=out_specs, check_vma=False
    )
```

```python
import functools

import jax
import jax.numpy as jnp
from jax import lax
from jax.experimental import pallas as pl
from jax.experimental.pallas import tpu as pltpu
from jax.sharding import PartitionSpec as P

HD = 128
SPAN = 512
PREFILLS = 2
TILE = 256
NEGATIVE = -1e30
THETA = 1000000.0
EPSILON = 1e-06
SCALE = HD ** (-0.5)


def rotate(values, places):
    half_dim = values.shape[-1] // 2
    frequency = THETA ** (-jnp.arange(half_dim, dtype=jnp.float32) / half_dim)
    angles = places.astype(jnp.float32)[:, None] * frequency[None, :]
    cosine = jnp.cos(angles)[:, None, :]
    sine_part = jnp.sin(angles)[:, None, :]
    front_half = values[..., :half_dim]
    second = values[..., half_dim:]
    return jnp.concatenate(
        [front_half * cosine - second * sine_part, second * cosine + front_half * sine_part],
        axis=-1,
    )


def nt_dot(a, b):
    return lax.dot_general(a, b, (((1,), (1,)), ((), ())), preferred_element_type=jnp.float32)


def tn_dot(a, b):
    return lax.dot_general(a, b, (((0,), (0,)), ((), ())), preferred_element_type=jnp.float32)


def tile_step(q, k, v, lo, hi, first, state, top_ref, sum_ref, acc_ref, width):
    scores = nt_dot(k, q) * SCALE
    index = first + lax.broadcasted_iota(jnp.int32, scores.shape, 0)
    visible = (index >= lo) & (index < hi)
    scores = jnp.where(visible, scores, NEGATIVE)
    old = top_ref[:, :width]
    top = jnp.maximum(old, jnp.max(scores, axis=0, keepdims=True))
    weights = jnp.where(visible, jnp.exp(scores - top), 0.0)
    factor = jnp.exp(old - top)
    top_ref[:, :width] = top
    sum_ref[:, :width] = sum_ref[:, :width] * factor + jnp.sum(weights, axis=0, keepdims=True)
    acc_ref[:, :width] = acc_ref[:, :width] * factor + tn_dot(v, weights.astype(jnp.bfloat16))


def begin(top_ref, sum_ref, acc_ref):
    top_ref[...] = jnp.full(top_ref.shape, NEGATIVE, jnp.float32)
    sum_ref[...] = jnp.zeros(sum_ref.shape, jnp.float32)
    acc_ref[...] = jnp.zeros(acc_ref.shape, jnp.float32)


def finish(top_ref, sum_ref, acc_ref, width):
    total = sum_ref[:, :width]
    some = total > 0.0
    safe = jnp.where(some, total, 1.0)
    out = acc_ref[:, :width] / safe
    return out, jnp.where(some, top_ref[:, :width] + jnp.log(safe), NEGATIVE)


def unpack(source, target):
    rows = target.shape[0] // source.shape[0]
    for block in range(source.shape[0]):
        target[block * rows:(block + 1) * rows, :] = source[block, :rows, :].astype(jnp.float32)


def cache_kernel(
    range_ref, lo_ref, hi_ref, blocks_ref, k_ref, v_ref, o_ref, l_ref, top_ref, sum_ref, acc_ref, q_ref
):
    groups = q_ref.shape[1] // HD
    boundary = PREFILLS * SPAN
    decodes = q_ref.shape[0] - boundary
    unpack(blocks_ref, q_ref)

    def attend(q, lo, hi, first_tile, last_tile, width):
        begin(top_ref, sum_ref, acc_ref)

        @pl.loop(first_tile, last_tile)
        def _(tile):
            first = pl.multiple_of(tile * TILE, TILE)
            tile_step(
                q, k_ref[pl.ds(first, TILE), :], v_ref[pl.ds(first, TILE), :],
                lo, hi, first, None, top_ref, sum_ref, acc_ref, width,
            )

        return finish(top_ref, sum_ref, acc_ref, width)

    q = jnp.concatenate(
        [q_ref[boundary:, g * HD:(g + 1) * HD] for g in range(groups)], axis=0
    ).astype(jnp.bfloat16)
    scores = nt_dot(k_ref[...], q) * SCALE
    index = lax.broadcasted_iota(jnp.int32, scores.shape, 0)
    visible = (index >= lo_ref[...]) & (index < hi_ref[...])
    scores = jnp.where(visible, scores, NEGATIVE)
    top = jnp.max(scores, axis=0, keepdims=True)
    weights = jnp.where(visible, jnp.exp(scores - top), 0.0)
    total = jnp.sum(weights, axis=0, keepdims=True)
    some = total > 0.0
    safe = jnp.where(some, total, 1.0)
    out = tn_dot(v_ref[...], weights.astype(jnp.bfloat16)) / safe
    lse = jnp.where(some, top + jnp.log(safe), NEGATIVE)
    out = out.T.astype(jnp.bfloat16)
    for g in range(groups):
        o_ref[boundary:, g * HD:(g + 1) * HD] = out[g * decodes:(g + 1) * decodes]
        l_ref[0, g:g + 1, boundary:] = lse[:, g * decodes:(g + 1) * decodes]
    for r in range(PREFILLS):
        lo, hi = range_ref[2 * r], range_ref[2 * r + 1]
        rows = slice(r * SPAN, (r + 1) * SPAN)

        @pl.when(hi > lo)
        def _():
            for g in range(groups):
                q = q_ref[rows, g * HD:(g + 1) * HD].astype(jnp.bfloat16)
                out, lse = attend(q, lo, hi, lo // TILE, (hi + TILE - 1) // TILE, SPAN)
                o_ref[rows, g * HD:(g + 1) * HD] = out.T.astype(jnp.bfloat16)
                l_ref[0, g:g + 1, rows] = lse

        @pl.when(hi <= lo)
        def _():
            o_ref[rows, :] = jnp.zeros((SPAN, groups * HD), jnp.bfloat16)
            l_ref[0, :, rows] = jnp.full((groups, SPAN), NEGATIVE, jnp.float32)


def cache_attention(rows, ranges, lo, hi, queries, keys, values):
    count, padded, q_width = queries.shape
    slots, kv_width = keys.shape
    kv_heads = kv_width // HD
    groups = q_width // kv_width
    whole = lambda c: (0, 0)
    column = lambda c: (0, c)
    return pl.pallas_call(
        cache_kernel,
        name="cache_attention",
        grid=(kv_heads,),
        out_shape=(
            jax.ShapeDtypeStruct((rows, q_width), jnp.bfloat16),
            jax.ShapeDtypeStruct((kv_heads, groups, rows), jnp.float32),
        ),
        in_specs=[
            pl.BlockSpec(memory_space=pltpu.SMEM),
            pl.BlockSpec(lo.shape, whole),
            pl.BlockSpec(hi.shape, whole),
            pl.BlockSpec((count, padded, groups * HD), lambda c: (0, 0, c)),
            pl.BlockSpec((slots, HD), column),
            pl.BlockSpec((slots, HD), column),
        ],
        out_specs=(
            pl.BlockSpec((rows, groups * HD), column),
            pl.BlockSpec((1, groups, rows), lambda c: (c, 0, 0)),
        ),
        scratch_shapes=[
            pltpu.VMEM((1, SPAN), jnp.float32),
            pltpu.VMEM((1, SPAN), jnp.float32),
            pltpu.VMEM((HD, SPAN), jnp.float32),
            pltpu.VMEM((rows, groups * HD), jnp.float32),
        ],
        compiler_params=pltpu.CompilerParams(vmem_limit_bytes=32 << 20),
        cost_estimate=pl.CostEstimate(
            flops=4 * slots * q_width * 512, bytes_accessed=8 << 20, transcendentals=1 << 20
        ),
    )(ranges, lo, hi, queries, keys, values)


def self_kernel(lo_ref, hi_ref, q_ref, k_ref, v_ref, o_ref, l_ref, keys_ref, values_ref):
    groups = q_ref.shape[1] // HD
    unpack(k_ref, keys_ref)
    unpack(v_ref, values_ref)
    keys = keys_ref[...].astype(jnp.bfloat16)
    values = values_ref[...].astype(jnp.bfloat16)
    for g in range(groups):
        scores = nt_dot(keys, q_ref[:, g * HD:(g + 1) * HD]) * SCALE
        index = lax.broadcasted_iota(jnp.int32, scores.shape, 0)
        visible = (index >= lo_ref[...]) & (index <= hi_ref[...])
        scores = jnp.where(visible, scores, NEGATIVE)
        top = jnp.max(scores, axis=0, keepdims=True)
        weights = jnp.where(visible, jnp.exp(scores - top), 0.0)
        total = jnp.sum(weights, axis=0, keepdims=True)
        out = tn_dot(values, weights.astype(jnp.bfloat16)) / total
        o_ref[:, g * HD:(g + 1) * HD] = out.T
        l_ref[0, g:g + 1, :] = top + jnp.log(total)


def self_attention(lo, hi, queries, new):
    rows, q_width = queries.shape
    blocks, block_rows, width = new.shape
    count = blocks * block_rows
    kv_heads = width // (2 * HD)
    groups = q_width // HD // kv_heads
    return pl.pallas_call(
        self_kernel,
        name="new_row_attention",
        grid=(kv_heads,),
        out_shape=(
            jax.ShapeDtypeStruct((rows, q_width), jnp.float32),
            jax.ShapeDtypeStruct((kv_heads, groups, rows), jnp.float32),
        ),
        in_specs=[
            pl.BlockSpec(lo.shape, lambda c: (0, 0)),
            pl.BlockSpec(hi.shape, lambda c: (0, 0)),
            pl.BlockSpec((rows, groups * HD), lambda c: (0, c)),
            pl.BlockSpec((blocks, block_rows, HD), lambda c: (0, 0, c)),
            pl.BlockSpec((blocks, block_rows, HD), lambda c: (0, 0, kv_heads + c)),
        ],
        out_specs=(
            pl.BlockSpec((rows, groups * HD), lambda c: (0, c)),
            pl.BlockSpec((1, groups, rows), lambda c: (c, 0, 0)),
        ),
        scratch_shapes=[pltpu.VMEM((count, HD), jnp.float32)] * 2,
        compiler_params=pltpu.CompilerParams(vmem_limit_bytes=32 << 20),
        cost_estimate=pl.CostEstimate(
            flops=4 * count * q_width * rows, bytes_accessed=4 << 20, transcendentals=1 << 20
        ),
    )(lo, hi, queries, new, new)


def flip(index, bit):
    return index + bit - 2 * bit * ((index // bit) % 2)


def greet(peers):
    barrier = pltpu.get_barrier_semaphore()
    for peer in peers:
        pl.semaphore_signal(
            barrier,
            inc=1,
            device_id=(peer, lax.axis_index("tp")),
            device_id_type=pl.DeviceIdType.MESH,
        )
    pl.semaphore_wait(barrier, len(peers))


def offset_index(index, offset, bits):
    for bit in bits:
        if offset & bit:
            index = flip(index, bit)
    return index


def gather_kernel(bits, x_ref, out_ref, own_sem, send_sem, recv_sem):
    me = lax.axis_index("seq")
    greet([flip(me, bit) for bit in bits])
    half = x_ref.shape[1] // 2
    orders = [list(bits), list(bits[:-2]) + [bits[-1], bits[-2]]]
    own = pltpu.make_async_copy(x_ref, out_ref.at[me], own_sem)
    own.start()
    held = [[0], [0]]
    sends, got, number = [], {}, [0, 0]
    for step in range(len(bits)):
        fresh = [[], []]
        for place in range(len(held[0])):
            for part in range(2):
                bit, offset = orders[part][step], held[part][place]
                columns = pl.ds(part * half, half)
                if offset and (part, offset) in got:
                    got.pop((part, offset)).wait_recv()
                block = offset_index(me, offset, bits)
                copy = pltpu.make_async_remote_copy(
                    src_ref=out_ref.at[block, :, columns] if offset else x_ref.at[:, columns],
                    dst_ref=out_ref.at[block, :, columns],
                    send_sem=send_sem.at[part, number[part]],
                    recv_sem=recv_sem.at[part, offset ^ bit],
                    device_id=(flip(me, bit), lax.axis_index("tp")),
                    device_id_type=pl.DeviceIdType.MESH,
                )
                copy.start()
                number[part] += 1
                sends.append(copy)
                fresh[part].append((offset ^ bit, copy))
        for part in range(2):
            for offset, copy in fresh[part]:
                held[part].append(offset)
                got[(part, offset)] = copy
    for copy in got.values():
        copy.wait_recv()
    for copy in sends:
        copy.wait_send()
    own.wait()


def gather(block, count):
    bits = []
    while 1 << len(bits) < count:
        bits.insert(0, 1 << len(bits))
    return pl.pallas_call(
        functools.partial(gather_kernel, bits),
        name="gather_rows",
        out_shape=jax.ShapeDtypeStruct((count,) + block.shape, block.dtype),
        in_specs=[pl.BlockSpec(memory_space=pl.ANY)],
        out_specs=pl.BlockSpec(memory_space=pl.ANY),
        scratch_shapes=[
            pltpu.SemaphoreType.DMA,
            pltpu.SemaphoreType.DMA((2, count - 1)),
            pltpu.SemaphoreType.DMA((2, count)),
        ],
        compiler_params=pltpu.CompilerParams(collective_id=0, has_side_effects=True),
        cost_estimate=pl.CostEstimate(
            flops=0, bytes_accessed=100 << 20, transcendentals=0
        ),
    )(block)


def exchange_kernel(count, x_ref, l_ref, out_ref, lout_ref, own_sem, send_sem, recv_sem):
    me = lax.axis_index("seq")
    peers = [lax.rem(me + k, count) for k in range(1, count)]
    greet(peers)
    own = pltpu.make_async_copy(x_ref.at[me], out_ref.at[me], own_sem.at[0])
    own_lse = pltpu.make_async_copy(l_ref.at[me], lout_ref.at[me], own_sem.at[1])
    own.start()
    own_lse.start()
    copies = []
    for k in range(1, count):
        for part, (source, target) in enumerate(((x_ref, out_ref), (l_ref, lout_ref))):
            copy = pltpu.make_async_remote_copy(
                src_ref=source.at[peers[k - 1]],
                dst_ref=target.at[me],
                send_sem=send_sem.at[part, k],
                recv_sem=recv_sem.at[part, k],
                device_id=(peers[k - 1], lax.axis_index("tp")),
                device_id_type=pl.DeviceIdType.MESH,
            )
            copy.start()
            copies.append((part, k, copy))
    for part, k, copy in copies:
        copy.wait_send()
        copy.wait_recv()
    own.wait()
    own_lse.wait()


def exchange(blocks, lse):
    count = blocks.shape[0]
    any_spec = pl.BlockSpec(memory_space=pl.ANY)
    return pl.pallas_call(
        functools.partial(exchange_kernel, count),
        name="exchange_partials",
        out_shape=(
            jax.ShapeDtypeStruct(blocks.shape, blocks.dtype),
            jax.ShapeDtypeStruct(lse.shape, lse.dtype),
        ),
        in_specs=[any_spec, any_spec],
        out_specs=(any_spec, any_spec),
        scratch_shapes=[
            pltpu.SemaphoreType.DMA((2,)),
            pltpu.SemaphoreType.DMA((2, count)),
            pltpu.SemaphoreType.DMA((2, count)),
        ],
        compiler_params=pltpu.CompilerParams(collective_id=1, has_side_effects=True),
        cost_estimate=pl.CostEstimate(
            flops=0, bytes_accessed=160 << 20, transcendentals=0
        ),
    )(blocks, lse)


def project_kernel(count, a_ref, w_ref, o_ref, send_ref, recv_ref, send_sem, recv_sem):
    me = lax.axis_index("tp")
    columns = o_ref.shape[1]
    peers = [lax.rem(me + k, count) for k in range(1, count)]
    barrier = pltpu.get_barrier_semaphore()
    for peer in peers:
        pl.semaphore_signal(
            barrier,
            inc=1,
            device_id=(lax.axis_index("seq"), peer),
            device_id_type=pl.DeviceIdType.MESH,
        )
    def product(owner):
        return jnp.dot(
            a_ref[...],
            w_ref[:, pl.ds(pl.multiple_of(owner * columns, columns), columns)],
            preferred_element_type=jnp.float32,
        )

    copies = []
    for k in range(1, count):
        send_ref[k - 1] = product(peers[k - 1]).astype(jnp.bfloat16)
        if k == 1:
            pl.semaphore_wait(barrier, count - 1)
        copy = pltpu.make_async_remote_copy(
            src_ref=send_ref.at[k - 1],
            dst_ref=recv_ref.at[k - 1],
            send_sem=send_sem.at[k - 1],
            recv_sem=recv_sem.at[k - 1],
            device_id=(lax.axis_index("seq"), peers[k - 1]),
            device_id_type=pl.DeviceIdType.MESH,
        )
        copy.start()
        copies.append(copy)
    total = product(me)
    for k, copy in enumerate(copies):
        copy.wait_recv()
        total = total + recv_ref[k].astype(jnp.float32)
    o_ref[...] = total.astype(jnp.bfloat16)
    for copy in copies:
        copy.wait_send()


def project(attended, w_out, count):
    rows = attended.shape[0]
    columns = w_out.shape[1] // count
    vmem = pl.BlockSpec(memory_space=pltpu.VMEM)
    return pl.pallas_call(
        functools.partial(project_kernel, count),
        name="project_and_add",
        out_shape=jax.ShapeDtypeStruct((rows, columns), jnp.bfloat16),
        in_specs=[vmem, vmem],
        out_specs=vmem,
        scratch_shapes=[
            pltpu.VMEM((count - 1, rows, columns), jnp.bfloat16),
            pltpu.VMEM((count - 1, rows, columns), jnp.bfloat16),
            pltpu.SemaphoreType.DMA((count - 1,)),
            pltpu.SemaphoreType.DMA((count - 1,)),
        ],
        compiler_params=pltpu.CompilerParams(
            collective_id=2, has_side_effects=True, vmem_limit_bytes=24 << 20
        ),
        cost_estimate=pl.CostEstimate(
            flops=2 * rows * w_out.size, bytes_accessed=8 << 20, transcendentals=0
        ),
    )(attended, w_out)


def flat_blocks(values, count, flat):
    values = values.reshape(count, -1, HD)
    return jnp.pad(values, ((0, 0), (0, flat - values.shape[1]), (0, 0)))


def per_device(
    tokens,
    norm_gain,
    w_query,
    w_key,
    w_value,
    w_out,
    cache_keys,
    cache_values,
    cached_len,
    block_of_shard,
):
    seq_count = lax.axis_size("seq")
    seq_index = lax.axis_index("seq")
    tok_rows = tokens.shape[0]
    all_rows = tok_rows * seq_count
    q_heads = w_query.shape[1] // HD
    kv_heads = w_key.shape[1] // HD
    groups = q_heads // kv_heads
    slots = cache_keys.shape[0]
    requests = cached_len.shape[0]
    boundary = PREFILLS * SPAN

    number = jnp.arange(requests, dtype=jnp.int32)
    ends = jnp.sum(jnp.where(number[None, :] <= number[:, None], cached_len[None, :], 0), axis=1)
    base = block_of_shard[0] * slots
    lows = jnp.clip(ends - cached_len - base, 0, slots)
    highs = jnp.clip(ends - base, 0, slots)
    ranges = jnp.stack([lows[:PREFILLS], highs[:PREFILLS]], axis=1).reshape(-1)
    decode_lo = jnp.tile(lows[PREFILLS:], groups)[None, :]
    decode_hi = jnp.tile(highs[PREFILLS:], groups)[None, :]

    my_rows = seq_index * tok_rows + jnp.arange(tok_rows, dtype=jnp.int32)
    prefill = my_rows < boundary
    my_request = jnp.where(prefill, my_rows // SPAN, PREFILLS + my_rows - boundary)
    my_begin = jnp.sum(
        jnp.where(my_request[:, None] == number[None, :], cached_len[None, :], 0), axis=1
    )
    my_position = my_begin + jnp.where(prefill, my_rows % SPAN, 0)

    hidden = tokens.astype(jnp.float32)
    scale_row = lax.rsqrt(jnp.mean(hidden * hidden, axis=1, keepdims=True) + EPSILON)
    normed = (hidden * scale_row * norm_gain.astype(jnp.float32)[None, :]).astype(jnp.bfloat16)
    queries = jnp.dot(normed, w_query, preferred_element_type=jnp.float32).reshape(
        tok_rows, q_heads, HD
    )
    queries = rotate(queries, my_position).astype(jnp.bfloat16).reshape(tok_rows, q_heads * HD)
    new_keys = jnp.dot(normed, w_key, preferred_element_type=jnp.float32).reshape(
        tok_rows, kv_heads, HD
    )
    new_keys = rotate(new_keys, my_position).astype(jnp.bfloat16).reshape(tok_rows, kv_heads * HD)
    new_values = jnp.dot(normed, w_value, preferred_element_type=jnp.float32).astype(jnp.bfloat16)
    lines = tok_rows * q_heads
    flat = -(-lines // 16) * 16
    gathered = gather(
        jnp.pad(queries, ((0, -(-tok_rows // 16) * 16 - tok_rows), (0, 0))), seq_count
    )
    new = lax.all_gather(jnp.concatenate([new_keys, new_values], axis=1), "seq", axis=0)

    part, part_lse = cache_attention(
        all_rows, ranges, decode_lo, decode_hi, gathered, cache_keys, cache_values
    )
    part_lse = part_lse.reshape(q_heads, seq_count, tok_rows).transpose(1, 0, 2)
    lanes = -(-tok_rows // 128) * 128
    head_rows = -(-q_heads // 8) * 8
    part_lse = jnp.pad(
        part_lse, ((0, 0), (0, head_rows - q_heads), (0, lanes - tok_rows))
    )
    parts, parts_lse = exchange(flat_blocks(part, seq_count, flat), part_lse)
    parts = parts[:, :lines].reshape(seq_count, tok_rows, q_heads, HD)
    parts_lse = parts_lse[:, :q_heads, :tok_rows].transpose(0, 2, 1)

    padded = -(-tok_rows // 128) * 128
    lane_rows = seq_index * tok_rows + jnp.minimum(
        jnp.arange(padded, dtype=jnp.int32), tok_rows - 1
    )
    first_key = jnp.where(lane_rows < boundary, lane_rows // SPAN * SPAN, lane_rows)
    own, own_lse = self_attention(
        first_key[None, :],
        lane_rows[None, :],
        jnp.pad(queries, ((0, padded - tok_rows), (0, 0))),
        new,
    )
    own = own[:tok_rows].reshape(tok_rows, q_heads, HD)
    own_lse = own_lse.reshape(q_heads, padded)[:, :tok_rows].T
    top = jnp.maximum(own_lse, jnp.max(parts_lse, axis=0))
    own_weight = jnp.exp(own_lse - top)
    weights = jnp.exp(parts_lse - top[None])
    norm = own_weight + jnp.sum(weights, axis=0)
    cached = jnp.sum(parts.astype(jnp.float32) * weights[..., None], axis=0)
    attended = (own * own_weight[..., None] + cached) / norm[..., None]
    attended = attended.astype(jnp.bfloat16)
    attended = attended.reshape(tok_rows, q_heads * HD)
    attended = jnp.pad(attended, ((0, -(-tok_rows // 16) * 16 - tok_rows), (0, 0)))
    return project(attended, w_out, lax.axis_size("tp"))[:tok_rows]


def solution(mesh):
    in_specs = (
        P("seq", None),
        P(),
        P(None, "tp"),
        P(None, "tp"),
        P(None, "tp"),
        P("tp", None),
        P("seq", "tp"),
        P("seq", "tp"),
        P(),
        P("seq"),
    )
    out_specs = P("seq", "tp")
    return jax.shard_map(
        per_device, mesh=mesh, in_specs=in_specs, out_specs=out_specs, check_vma=False
    )
```

```python
import functools

import jax
import jax.numpy as jnp
from jax import lax
from jax.experimental import pallas as pl
from jax.experimental.pallas import tpu as pltpu
from jax.sharding import PartitionSpec as P

HD = 128
SPAN = 512
PREFILLS = 2
TILE = 256
NEGATIVE = -1e30
THETA = 1000000.0
EPSILON = 1e-06
SCALE = HD ** (-0.5)


def rotate(values, places):
    half_dim = values.shape[-1] // 2
    frequency = THETA ** (-jnp.arange(half_dim, dtype=jnp.float32) / half_dim)
    angles = places.astype(jnp.float32)[:, None] * frequency[None, :]
    cosine = jnp.cos(angles)[:, None, :]
    sine_part = jnp.sin(angles)[:, None, :]
    front_half = values[..., :half_dim]
    second = values[..., half_dim:]
    return jnp.concatenate(
        [front_half * cosine - second * sine_part, second * cosine + front_half * sine_part],
        axis=-1,
    )


def nt_dot(a, b):
    return lax.dot_general(a, b, (((1,), (1,)), ((), ())), preferred_element_type=jnp.float32)


def tn_dot(a, b):
    return lax.dot_general(a, b, (((0,), (0,)), ((), ())), preferred_element_type=jnp.float32)


def tile_step(q, k, v, lo, hi, first, state, top_ref, sum_ref, acc_ref, width):
    scores = nt_dot(k, q) * SCALE
    index = first + lax.broadcasted_iota(jnp.int32, scores.shape, 0)
    visible = (index >= lo) & (index < hi)
    scores = jnp.where(visible, scores, NEGATIVE)
    old = top_ref[:, :width]
    top = jnp.maximum(old, jnp.max(scores, axis=0, keepdims=True))
    weights = jnp.where(visible, jnp.exp(scores - top), 0.0)
    factor = jnp.exp(old - top)
    top_ref[:, :width] = top
    sum_ref[:, :width] = sum_ref[:, :width] * factor + jnp.sum(weights, axis=0, keepdims=True)
    acc_ref[:, :width] = acc_ref[:, :width] * factor + tn_dot(v, weights.astype(jnp.bfloat16))


def begin(top_ref, sum_ref, acc_ref):
    top_ref[...] = jnp.full(top_ref.shape, NEGATIVE, jnp.float32)
    sum_ref[...] = jnp.zeros(sum_ref.shape, jnp.float32)
    acc_ref[...] = jnp.zeros(acc_ref.shape, jnp.float32)


def finish(top_ref, sum_ref, acc_ref, width):
    total = sum_ref[:, :width]
    some = total > 0.0
    safe = jnp.where(some, total, 1.0)
    out = acc_ref[:, :width] / safe
    return out, jnp.where(some, top_ref[:, :width] + jnp.log(safe), NEGATIVE)


def unpack(source, target):
    rows = target.shape[0] // source.shape[0]
    for block in range(source.shape[0]):
        target[block * rows:(block + 1) * rows, :] = source[block, :rows, :].astype(jnp.float32)


def cache_kernel(
    range_ref, lo_ref, hi_ref, blocks_ref, k_ref, v_ref, o_ref, l_ref, top_ref, sum_ref, acc_ref, q_ref
):
    groups = q_ref.shape[1] // HD
    boundary = PREFILLS * SPAN
    decodes = q_ref.shape[0] - boundary
    unpack(blocks_ref, q_ref)

    def attend(q, lo, hi, first_tile, last_tile, width):
        begin(top_ref, sum_ref, acc_ref)

        @pl.loop(first_tile, last_tile)
        def _(tile):
            first = pl.multiple_of(tile * TILE, TILE)
            tile_step(
                q, k_ref[pl.ds(first, TILE), :], v_ref[pl.ds(first, TILE), :],
                lo, hi, first, None, top_ref, sum_ref, acc_ref, width,
            )

        return finish(top_ref, sum_ref, acc_ref, width)

    q = jnp.concatenate(
        [q_ref[boundary:, g * HD:(g + 1) * HD] for g in range(groups)], axis=0
    ).astype(jnp.bfloat16)
    scores = nt_dot(k_ref[...], q) * SCALE
    index = lax.broadcasted_iota(jnp.int32, scores.shape, 0)
    visible = (index >= lo_ref[...]) & (index < hi_ref[...])
    scores = jnp.where(visible, scores, NEGATIVE)
    top = jnp.max(scores, axis=0, keepdims=True)
    weights = jnp.where(visible, jnp.exp(scores - top), 0.0)
    total = jnp.sum(weights, axis=0, keepdims=True)
    some = total > 0.0
    safe = jnp.where(some, total, 1.0)
    out = tn_dot(v_ref[...], weights.astype(jnp.bfloat16)) / safe
    lse = jnp.where(some, top + jnp.log(safe), NEGATIVE)
    out = out.T.astype(jnp.bfloat16)
    for g in range(groups):
        o_ref[boundary:, g * HD:(g + 1) * HD] = out[g * decodes:(g + 1) * decodes]
        l_ref[0, g:g + 1, boundary:] = lse[:, g * decodes:(g + 1) * decodes]
    for r in range(PREFILLS):
        lo, hi = range_ref[2 * r], range_ref[2 * r + 1]
        rows = slice(r * SPAN, (r + 1) * SPAN)

        @pl.when(hi > lo)
        def _():
            q = jnp.concatenate(
                [q_ref[rows, g * HD:(g + 1) * HD] for g in range(groups)], axis=0
            ).astype(jnp.bfloat16)
            out, lse = attend(q, lo, hi, lo // TILE, (hi + TILE - 1) // TILE, groups * SPAN)
            out = out.T.astype(jnp.bfloat16)
            for g in range(groups):
                o_ref[rows, g * HD:(g + 1) * HD] = out[g * SPAN:(g + 1) * SPAN]
                l_ref[0, g:g + 1, rows] = lse[:, g * SPAN:(g + 1) * SPAN]

        @pl.when(hi <= lo)
        def _():
            o_ref[rows, :] = jnp.zeros((SPAN, groups * HD), jnp.bfloat16)
            l_ref[0, :, rows] = jnp.full((groups, SPAN), NEGATIVE, jnp.float32)


def cache_attention(rows, ranges, lo, hi, queries, keys, values):
    count, padded, q_width = queries.shape
    slots, kv_width = keys.shape
    kv_heads = kv_width // HD
    groups = q_width // kv_width
    whole = lambda c: (0, 0)
    column = lambda c: (0, c)
    return pl.pallas_call(
        cache_kernel,
        name="cache_attention",
        grid=(kv_heads,),
        out_shape=(
            jax.ShapeDtypeStruct((rows, q_width), jnp.bfloat16),
            jax.ShapeDtypeStruct((kv_heads, groups, rows), jnp.float32),
        ),
        in_specs=[
            pl.BlockSpec(memory_space=pltpu.SMEM),
            pl.BlockSpec(lo.shape, whole),
            pl.BlockSpec(hi.shape, whole),
            pl.BlockSpec((count, padded, groups * HD), lambda c: (0, 0, c)),
            pl.BlockSpec((slots, HD), column),
            pl.BlockSpec((slots, HD), column),
        ],
        out_specs=(
            pl.BlockSpec((rows, groups * HD), column),
            pl.BlockSpec((1, groups, rows), lambda c: (c, 0, 0)),
        ),
        scratch_shapes=[
            pltpu.VMEM((1, groups * SPAN), jnp.float32),
            pltpu.VMEM((1, groups * SPAN), jnp.float32),
            pltpu.VMEM((HD, groups * SPAN), jnp.float32),
            pltpu.VMEM((rows, groups * HD), jnp.float32),
        ],
        compiler_params=pltpu.CompilerParams(vmem_limit_bytes=32 << 20),
        cost_estimate=pl.CostEstimate(
            flops=4 * slots * q_width * 512, bytes_accessed=8 << 20, transcendentals=1 << 20
        ),
    )(ranges, lo, hi, queries, keys, values)


def self_kernel(lo_ref, hi_ref, q_ref, k_ref, v_ref, o_ref, l_ref, keys_ref, values_ref):
    groups = q_ref.shape[1] // HD
    unpack(k_ref, keys_ref)
    unpack(v_ref, values_ref)
    keys = keys_ref[...].astype(jnp.bfloat16)
    values = values_ref[...].astype(jnp.bfloat16)
    for g in range(groups):
        scores = nt_dot(keys, q_ref[:, g * HD:(g + 1) * HD]) * SCALE
        index = lax.broadcasted_iota(jnp.int32, scores.shape, 0)
        visible = (index >= lo_ref[...]) & (index <= hi_ref[...])
        scores = jnp.where(visible, scores, NEGATIVE)
        top = jnp.max(scores, axis=0, keepdims=True)
        weights = jnp.where(visible, jnp.exp(scores - top), 0.0)
        total = jnp.sum(weights, axis=0, keepdims=True)
        out = tn_dot(values, weights.astype(jnp.bfloat16)) / total
        o_ref[:, g * HD:(g + 1) * HD] = out.T
        l_ref[0, g:g + 1, :] = top + jnp.log(total)


def self_attention(lo, hi, queries, new):
    rows, q_width = queries.shape
    blocks, block_rows, width = new.shape
    count = blocks * block_rows
    kv_heads = width // (2 * HD)
    groups = q_width // HD // kv_heads
    return pl.pallas_call(
        self_kernel,
        name="new_row_attention",
        grid=(kv_heads,),
        out_shape=(
            jax.ShapeDtypeStruct((rows, q_width), jnp.float32),
            jax.ShapeDtypeStruct((kv_heads, groups, rows), jnp.float32),
        ),
        in_specs=[
            pl.BlockSpec(lo.shape, lambda c: (0, 0)),
            pl.BlockSpec(hi.shape, lambda c: (0, 0)),
            pl.BlockSpec((rows, groups * HD), lambda c: (0, c)),
            pl.BlockSpec((blocks, block_rows, HD), lambda c: (0, 0, c)),
            pl.BlockSpec((blocks, block_rows, HD), lambda c: (0, 0, kv_heads + c)),
        ],
        out_specs=(
            pl.BlockSpec((rows, groups * HD), lambda c: (0, c)),
            pl.BlockSpec((1, groups, rows), lambda c: (c, 0, 0)),
        ),
        scratch_shapes=[pltpu.VMEM((count, HD), jnp.float32)] * 2,
        compiler_params=pltpu.CompilerParams(vmem_limit_bytes=32 << 20),
        cost_estimate=pl.CostEstimate(
            flops=4 * count * q_width * rows, bytes_accessed=4 << 20, transcendentals=1 << 20
        ),
    )(lo, hi, queries, new, new)


def flip(index, bit):
    return index + bit - 2 * bit * ((index // bit) % 2)


def greet(peers):
    barrier = pltpu.get_barrier_semaphore()
    for peer in peers:
        pl.semaphore_signal(
            barrier,
            inc=1,
            device_id=(peer, lax.axis_index("tp")),
            device_id_type=pl.DeviceIdType.MESH,
        )
    pl.semaphore_wait(barrier, len(peers))


def offset_index(index, offset, bits):
    for bit in bits:
        if offset & bit:
            index = flip(index, bit)
    return index


def gather_kernel(bits, x_ref, out_ref, own_sem, send_sem, recv_sem):
    me = lax.axis_index("seq")
    greet([flip(me, bit) for bit in bits])
    half = x_ref.shape[1] // 2
    orders = [list(bits), list(bits[:-2]) + [bits[-1], bits[-2]]]
    own = pltpu.make_async_copy(x_ref, out_ref.at[me], own_sem)
    own.start()
    held = [[0], [0]]
    sends, got, number = [], {}, [0, 0]
    for step in range(len(bits)):
        fresh = [[], []]
        for place in range(len(held[0])):
            for part in range(2):
                bit, offset = orders[part][step], held[part][place]
                columns = pl.ds(part * half, half)
                if offset and (part, offset) in got:
                    got.pop((part, offset)).wait_recv()
                block = offset_index(me, offset, bits)
                copy = pltpu.make_async_remote_copy(
                    src_ref=out_ref.at[block, :, columns] if offset else x_ref.at[:, columns],
                    dst_ref=out_ref.at[block, :, columns],
                    send_sem=send_sem.at[part, number[part]],
                    recv_sem=recv_sem.at[part, offset ^ bit],
                    device_id=(flip(me, bit), lax.axis_index("tp")),
                    device_id_type=pl.DeviceIdType.MESH,
                )
                copy.start()
                number[part] += 1
                sends.append(copy)
                fresh[part].append((offset ^ bit, copy))
        for part in range(2):
            for offset, copy in fresh[part]:
                held[part].append(offset)
                got[(part, offset)] = copy
    for copy in got.values():
        copy.wait_recv()
    for copy in sends:
        copy.wait_send()
    own.wait()


def gather(block, count):
    bits = []
    while 1 << len(bits) < count:
        bits.insert(0, 1 << len(bits))
    return pl.pallas_call(
        functools.partial(gather_kernel, bits),
        name="gather_rows",
        out_shape=jax.ShapeDtypeStruct((count,) + block.shape, block.dtype),
        in_specs=[pl.BlockSpec(memory_space=pl.ANY)],
        out_specs=pl.BlockSpec(memory_space=pl.ANY),
        scratch_shapes=[
            pltpu.SemaphoreType.DMA,
            pltpu.SemaphoreType.DMA((2, count - 1)),
            pltpu.SemaphoreType.DMA((2, count)),
        ],
        compiler_params=pltpu.CompilerParams(collective_id=0, has_side_effects=True),
        cost_estimate=pl.CostEstimate(
            flops=0, bytes_accessed=100 << 20, transcendentals=0
        ),
    )(block)


def exchange_kernel(count, x_ref, l_ref, out_ref, lout_ref, own_sem, send_sem, recv_sem):
    me = lax.axis_index("seq")
    peers = [lax.rem(me + k, count) for k in range(1, count)]
    greet(peers)
    own = pltpu.make_async_copy(x_ref.at[me], out_ref.at[me], own_sem.at[0])
    own_lse = pltpu.make_async_copy(l_ref.at[me], lout_ref.at[me], own_sem.at[1])
    own.start()
    own_lse.start()
    copies = []
    for k in range(1, count):
        for part, (source, target) in enumerate(((x_ref, out_ref), (l_ref, lout_ref))):
            copy = pltpu.make_async_remote_copy(
                src_ref=source.at[peers[k - 1]],
                dst_ref=target.at[me],
                send_sem=send_sem.at[part, k],
                recv_sem=recv_sem.at[part, k],
                device_id=(peers[k - 1], lax.axis_index("tp")),
                device_id_type=pl.DeviceIdType.MESH,
            )
            copy.start()
            copies.append((part, k, copy))
    for part, k, copy in copies:
        copy.wait_send()
        copy.wait_recv()
    own.wait()
    own_lse.wait()


def exchange(blocks, lse):
    count = blocks.shape[0]
    any_spec = pl.BlockSpec(memory_space=pl.ANY)
    return pl.pallas_call(
        functools.partial(exchange_kernel, count),
        name="exchange_partials",
        out_shape=(
            jax.ShapeDtypeStruct(blocks.shape, blocks.dtype),
            jax.ShapeDtypeStruct(lse.shape, lse.dtype),
        ),
        in_specs=[any_spec, any_spec],
        out_specs=(any_spec, any_spec),
        scratch_shapes=[
            pltpu.SemaphoreType.DMA((2,)),
            pltpu.SemaphoreType.DMA((2, count)),
            pltpu.SemaphoreType.DMA((2, count)),
        ],
        compiler_params=pltpu.CompilerParams(collective_id=1, has_side_effects=True),
        cost_estimate=pl.CostEstimate(
            flops=0, bytes_accessed=160 << 20, transcendentals=0
        ),
    )(blocks, lse)


def project_kernel(count, a_ref, w_ref, o_ref, send_ref, recv_ref, send_sem, recv_sem):
    me = lax.axis_index("tp")
    columns = o_ref.shape[1]
    peers = [lax.rem(me + k, count) for k in range(1, count)]
    barrier = pltpu.get_barrier_semaphore()
    for peer in peers:
        pl.semaphore_signal(
            barrier,
            inc=1,
            device_id=(lax.axis_index("seq"), peer),
            device_id_type=pl.DeviceIdType.MESH,
        )
    def product(owner):
        return jnp.dot(
            a_ref[...],
            w_ref[:, pl.ds(pl.multiple_of(owner * columns, columns), columns)],
            preferred_element_type=jnp.float32,
        )

    copies = []
    for k in range(1, count):
        send_ref[k - 1] = product(peers[k - 1]).astype(jnp.bfloat16)
        if k == 1:
            pl.semaphore_wait(barrier, count - 1)
        copy = pltpu.make_async_remote_copy(
            src_ref=send_ref.at[k - 1],
            dst_ref=recv_ref.at[k - 1],
            send_sem=send_sem.at[k - 1],
            recv_sem=recv_sem.at[k - 1],
            device_id=(lax.axis_index("seq"), peers[k - 1]),
            device_id_type=pl.DeviceIdType.MESH,
        )
        copy.start()
        copies.append(copy)
    total = product(me)
    for k, copy in enumerate(copies):
        copy.wait_recv()
        total = total + recv_ref[k].astype(jnp.float32)
    o_ref[...] = total.astype(jnp.bfloat16)
    for copy in copies:
        copy.wait_send()


def project(attended, w_out, count):
    rows = attended.shape[0]
    columns = w_out.shape[1] // count
    vmem = pl.BlockSpec(memory_space=pltpu.VMEM)
    return pl.pallas_call(
        functools.partial(project_kernel, count),
        name="project_and_add",
        out_shape=jax.ShapeDtypeStruct((rows, columns), jnp.bfloat16),
        in_specs=[vmem, vmem],
        out_specs=vmem,
        scratch_shapes=[
            pltpu.VMEM((count - 1, rows, columns), jnp.bfloat16),
            pltpu.VMEM((count - 1, rows, columns), jnp.bfloat16),
            pltpu.SemaphoreType.DMA((count - 1,)),
            pltpu.SemaphoreType.DMA((count - 1,)),
        ],
        compiler_params=pltpu.CompilerParams(
            collective_id=2, has_side_effects=True, vmem_limit_bytes=24 << 20
        ),
        cost_estimate=pl.CostEstimate(
            flops=2 * rows * w_out.size, bytes_accessed=8 << 20, transcendentals=0
        ),
    )(attended, w_out)


def flat_blocks(values, count, flat):
    values = values.reshape(count, -1, HD)
    return jnp.pad(values, ((0, 0), (0, flat - values.shape[1]), (0, 0)))


def per_device(
    tokens,
    norm_gain,
    w_query,
    w_key,
    w_value,
    w_out,
    cache_keys,
    cache_values,
    cached_len,
    block_of_shard,
):
    seq_count = lax.axis_size("seq")
    seq_index = lax.axis_index("seq")
    tok_rows = tokens.shape[0]
    all_rows = tok_rows * seq_count
    q_heads = w_query.shape[1] // HD
    kv_heads = w_key.shape[1] // HD
    groups = q_heads // kv_heads
    slots = cache_keys.shape[0]
    requests = cached_len.shape[0]
    boundary = PREFILLS * SPAN

    number = jnp.arange(requests, dtype=jnp.int32)
    ends = jnp.sum(jnp.where(number[None, :] <= number[:, None], cached_len[None, :], 0), axis=1)
    base = block_of_shard[0] * slots
    lows = jnp.clip(ends - cached_len - base, 0, slots)
    highs = jnp.clip(ends - base, 0, slots)
    ranges = jnp.stack([lows[:PREFILLS], highs[:PREFILLS]], axis=1).reshape(-1)
    decode_lo = jnp.tile(lows[PREFILLS:], groups)[None, :]
    decode_hi = jnp.tile(highs[PREFILLS:], groups)[None, :]

    my_rows = seq_index * tok_rows + jnp.arange(tok_rows, dtype=jnp.int32)
    prefill = my_rows < boundary
    my_request = jnp.where(prefill, my_rows // SPAN, PREFILLS + my_rows - boundary)
    my_begin = jnp.sum(
        jnp.where(my_request[:, None] == number[None, :], cached_len[None, :], 0), axis=1
    )
    my_position = my_begin + jnp.where(prefill, my_rows % SPAN, 0)

    hidden = tokens.astype(jnp.float32)
    scale_row = lax.rsqrt(jnp.mean(hidden * hidden, axis=1, keepdims=True) + EPSILON)
    normed = (hidden * scale_row * norm_gain.astype(jnp.float32)[None, :]).astype(jnp.bfloat16)
    queries = jnp.dot(normed, w_query, preferred_element_type=jnp.float32).reshape(
        tok_rows, q_heads, HD
    )
    queries = rotate(queries, my_position).astype(jnp.bfloat16).reshape(tok_rows, q_heads * HD)
    new_keys = jnp.dot(normed, w_key, preferred_element_type=jnp.float32).reshape(
        tok_rows, kv_heads, HD
    )
    new_keys = rotate(new_keys, my_position).astype(jnp.bfloat16).reshape(tok_rows, kv_heads * HD)
    new_values = jnp.dot(normed, w_value, preferred_element_type=jnp.float32).astype(jnp.bfloat16)
    lines = tok_rows * q_heads
    flat = -(-lines // 16) * 16
    gathered = gather(
        jnp.pad(queries, ((0, -(-tok_rows // 16) * 16 - tok_rows), (0, 0))), seq_count
    )
    new = lax.all_gather(jnp.concatenate([new_keys, new_values], axis=1), "seq", axis=0)

    part, part_lse = cache_attention(
        all_rows, ranges, decode_lo, decode_hi, gathered, cache_keys, cache_values
    )
    part_lse = part_lse.reshape(q_heads, seq_count, tok_rows).transpose(1, 0, 2)
    lanes = -(-tok_rows // 128) * 128
    head_rows = -(-q_heads // 8) * 8
    part_lse = jnp.pad(
        part_lse, ((0, 0), (0, head_rows - q_heads), (0, lanes - tok_rows))
    )
    parts, parts_lse = exchange(flat_blocks(part, seq_count, flat), part_lse)
    parts = parts[:, :lines].reshape(seq_count, tok_rows, q_heads, HD)
    parts_lse = parts_lse[:, :q_heads, :tok_rows].transpose(0, 2, 1)

    padded = -(-tok_rows // 128) * 128
    lane_rows = seq_index * tok_rows + jnp.minimum(
        jnp.arange(padded, dtype=jnp.int32), tok_rows - 1
    )
    first_key = jnp.where(lane_rows < boundary, lane_rows // SPAN * SPAN, lane_rows)
    own, own_lse = self_attention(
        first_key[None, :],
        lane_rows[None, :],
        jnp.pad(queries, ((0, padded - tok_rows), (0, 0))),
        new,
    )
    own = own[:tok_rows].reshape(tok_rows, q_heads, HD)
    own_lse = own_lse.reshape(q_heads, padded)[:, :tok_rows].T
    top = jnp.maximum(own_lse, jnp.max(parts_lse, axis=0))
    own_weight = jnp.exp(own_lse - top)
    weights = jnp.exp(parts_lse - top[None])
    norm = own_weight + jnp.sum(weights, axis=0)
    cached = jnp.sum(parts.astype(jnp.float32) * weights[..., None], axis=0)
    attended = (own * own_weight[..., None] + cached) / norm[..., None]
    attended = attended.astype(jnp.bfloat16)
    attended = attended.reshape(tok_rows, q_heads * HD)
    attended = jnp.pad(attended, ((0, -(-tok_rows // 16) * 16 - tok_rows), (0, 0)))
    return project(attended, w_out, lax.axis_size("tp"))[:tok_rows]


def solution(mesh):
    in_specs = (
        P("seq", None),
        P(),
        P(None, "tp"),
        P(None, "tp"),
        P(None, "tp"),
        P("tp", None),
        P("seq", "tp"),
        P("seq", "tp"),
        P(),
        P("seq"),
    )
    out_specs = P("seq", "tp")
    return jax.shard_map(
        per_device, mesh=mesh, in_specs=in_specs, out_specs=out_specs, check_vma=False
    )
```
